32 devices in a mesh: grp: 2 (over x), chan: 8 (over z, y), feed: 2 (over core).
Axes of the slice: x: 2, y: 2, z: 4, core: 2. Of those that a mesh axis runs over, the one named last changes fastest.
Arguments:
- voltages: int32 [2, 2048, 36608], P(None, ('grp', 'feed', 'chan')), parts along dimension 1, may hold values from -128 to 127, as said below
- input_order: int32 [1024], replicated, may hold values from 0 to 1023, each once
Outputs:
- visibility: float32 [2, 64, 1024, 1024], P(None, ('grp', 'chan'), 'feed'), parts along dimension 1
The draws below stay inside these ranges and needn't reach their ends.
There are 2 independent parts, one for each index of `grp`. The reference program is written for one: setup_inputs(seed, part) draws one part's arguments, and reference() takes and returns one part's arrays. A program takes and returns all parts, laid end to end along the dimension named above; an argument that names none is the same for every part. Nothing has to cross between parts.
Inputs may be any that keep to these rules, and one draw needn't show every extreme that they name: `voltages`: 8-bit digitizer samples, saturated at the ends of the range. `input_order`: each input of 0 to 1023 stands exactly once.
All inputs are finite; a program needn't handle non-finite values.
Results may differ from the reference program's by a relative error of at most 0.0039.
Values may be sent and summed in bfloat16 or wider, within the bound.
No kernel may reach another device: no remote copies, remote signals or barrier semaphores. Data moves between devices by JAX's collectives and lax.ppermute only.
A program may use at most 192 MiB of HBM per device.

```python
import math
import jax
import jax.numpy as jnp
from jax import lax

INPUT_COUNT = 1024
CH = 256
TAPS = 16
AVG = 8
SAMPLE_COUNT = 36608
CH_OUT = 32


source_count = 4


def draw_voltages(key, part):
    key = jax.random.fold_in(key, 7)
    gain_random_key, tone_random_key, quantizer_key, thermal_key, impulse_key, magnitude_key, polarity_key = jax.random.split(key, 7)
    level_table = jnp.array([20, 24, 29, 35, 42, 50, 60], dtype=jnp.int32)
    levels = level_table[jax.random.randint(quantizer_key, (INPUT_COUNT,), 0, 7)][None, :, None]
    noise_term = jax.random.randint(thermal_key, (2, INPUT_COUNT, SAMPLE_COUNT), -levels, levels + 1)
    gain_table = jax.random.randint(gain_random_key, (2, source_count, INPUT_COUNT), -1, 2)
    signals = jax.random.randint(tone_random_key, (2, source_count, SAMPLE_COUNT), -3, 4)
    real_part = noise_term[0]
    imag_part = noise_term[1]
    for source in range(source_count):
        gain_re = gain_table[0, source][:, None]
        gain_im = gain_table[1, source][:, None]
        signal_re = signals[0, source][None, :]
        signal_im = signals[1, source][None, :]
        real_part = real_part + gain_re * signal_re - gain_im * signal_im
        imag_part = imag_part + gain_re * signal_im + gain_im * signal_re
    added_total = jnp.stack([real_part, imag_part])
    impulse_mask = jax.random.randint(impulse_key, (2, INPUT_COUNT, SAMPLE_COUNT), 0, 1024) == 0
    impulse_magnitude = jax.random.randint(magnitude_key, (2, INPUT_COUNT, SAMPLE_COUNT), 150, 400)
    impulse_polarity = 2 * jax.random.randint(polarity_key, (2, INPUT_COUNT, SAMPLE_COUNT), 0, 2) - 1
    added_total = jnp.where(impulse_mask, added_total + impulse_polarity * impulse_magnitude, added_total)
    return jnp.clip(added_total, -128, 127).astype(jnp.int32)


def setup_inputs(seed: int = 0, part: int = 0) -> dict:
    streams_of = jax.random.split(jax.random.key(seed), 3)
    own_keys = jax.random.split(jax.random.fold_in(streams_of[2], part), 3)
    return {
        "voltages": draw_voltages(jax.random.fold_in(jax.random.fold_in(streams_of[2], part), 71), part),
        "input_order": jax.random.permutation(streams_of[1], INPUT_COUNT).astype(jnp.int32),
    }


def make_window():
    length = TAPS * CH
    position = jnp.arange(length, dtype=jnp.float32) + 0.5
    profile = jnp.sinc((position - length / 2) / CH) * (0.5 - 0.5 * jnp.cos(2 * math.pi * position / length))
    return profile.reshape(TAPS, CH)

def make_table():
    counter = jnp.arange(CH, dtype=jnp.int32)
    phases = counter[:, None] * counter[None, :] % CH
    angles = 2 * math.pi / CH * phases.astype(jnp.float32)
    cosine = jnp.cos(angles)
    sine_part = jnp.sin(angles)
    upper_rows = jnp.stack([cosine, -sine_part], axis=1)
    bottom = jnp.stack([sine_part, cosine], axis=1)
    return jnp.stack([upper_rows, bottom], axis=0).astype(jnp.bfloat16)

def polyphase(voltages, window):
    blocks = voltages.reshape(2, voltages.shape[1], -1, CH)
    frames = blocks.shape[2] - TAPS + 1
    running = window[0][None, None, None, :] * (blocks[:, :, 0:frames, :].astype(jnp.float32) / 64.0)
    for tap in range(1, TAPS):
        running = running + window[tap][None, None, None, :] * (blocks[:, :, tap:tap + frames, :].astype(jnp.float32) / 64.0)
    return running.astype(jnp.bfloat16)

def reference(voltages, input_order):
    window = make_window()
    table = make_table()
    filtered = polyphase(voltages, window)
    feed_count = voltages.shape[1]
    frames = filtered.shape[2]
    rows_in = jnp.transpose(filtered, (1, 2, 0, 3)).reshape(feed_count * frames, 2 * CH)
    product = jnp.dot(rows_in, table.reshape(2 * CH, 2 * CH), preferred_element_type=jnp.float32)
    spectra = (product * (1.0 / math.sqrt(CH))).astype(jnp.bfloat16).reshape(feed_count, frames, 2, CH)
    spectra = jnp.transpose(spectra, (0, 2, 3, 1))
    ordered = jnp.take(spectra, input_order, axis=0).reshape(feed_count, 2, CH_OUT, AVG, frames)
    norm_scale = 1.0 / (frames * AVG)

    def one_channel(out_index):
        picked = lax.dynamic_index_in_dim(ordered, out_index, 2, keepdims=False).astype(jnp.float32)
        twisted = jnp.stack([picked, jnp.concatenate([picked[:, 1:2], -picked[:, 0:1]], axis=1)])
        return jnp.einsum('sarck,brck->sab', twisted, picked, precision=lax.Precision.HIGHEST) * norm_scale
    stacked = lax.map(one_channel, jnp.arange(CH_OUT, dtype=jnp.int32))
    return jnp.transpose(stacked, (1, 0, 2, 3))
```

```python
import functools
import math

import jax
import jax.numpy as jnp
import numpy as np
from jax import lax
from jax.experimental import pallas as pl
from jax.experimental.pallas import tpu as pltpu
from jax.sharding import PartitionSpec as P

CH = 256
TAPS = 16
AVG = 8
LANES = 128
STEP = 16
COLS = 256
VMEM = 60 * 1024 * 1024
WINDOW = 5
NT = (((1,), (1,)), ((), ()))


def make_window():
    length = TAPS * CH
    position = np.arange(length, dtype=np.float64) + 0.5
    profile = np.sinc((position - length / 2) / CH) * (
        0.5 - 0.5 * np.cos(2 * math.pi * position / length)
    )
    profile = profile.astype(np.float32).reshape(TAPS, 1, CH) / np.float32(64 * math.sqrt(CH))
    return np.ascontiguousarray(np.broadcast_to(profile, (TAPS, 8, CH)))


def make_table():
    counter = np.arange(CH)
    angles = 2 * math.pi / CH * (counter[:, None] * counter[None, :] % CH)
    cosine, sine = np.cos(angles), np.sin(angles)
    table = np.stack(
        [np.concatenate([cosine, sine], axis=1), np.concatenate([-sine, cosine], axis=1)]
    )
    table = table.reshape(2, CH // AVG, AVG, 2 * CH).transpose(1, 0, 2, 3)
    return table.reshape(2 * CH, 2 * CH).astype(np.float32).astype(jnp.bfloat16)


def channelize_kernel(sizes, me_ref, va_ref, vb_ref, win_ref, tab_ref, *rest):
    feeds, chans, outs_per_dev, groups = sizes
    outs, (tabs, filt) = rest[:-2], rest[-2:]
    me = me_ref[0]
    span = LANES // feeds
    part = 2 * AVG * outs_per_dev

    @pl.when(pl.program_id(0) == 0)
    def _():
        for k in range(chans):
            start = pl.multiple_of((me ^ k) * part, part)
            tabs[k * part : (k + 1) * part, :] = tab_ref[pl.ds(start, part), :]

    flip = lax.rem(me, span)

    def strip(index, carry):
        f0 = pl.multiple_of(index * 16, 16)
        for p in range(2):
            for kk in range(CH // LANES):
                lanes = slice(kk * LANES, (kk + 1) * LANES)
                weights = [win_ref[tap, :, lanes] for tap in range(TAPS)]
                for t0 in range(0, STEP, 8):
                    total = [[None] * 8, [None] * 8]
                    for u in range(t0, t0 + 8 + TAPS - 1):
                        src = va_ref if u < STEP else vb_ref
                        col = (u % STEP) * CH + kk * LANES
                        both = src[p, pl.ds(f0, 16), col : col + LANES].astype(jnp.float32)
                        for half in range(2):
                            x = both[half * 8 : half * 8 + 8]
                            for t in range(8):
                                tap = u - t0 - t
                                if 0 <= tap < TAPS:
                                    term = weights[tap] * x
                                    old = total[half][t]
                                    total[half][t] = term if old is None else old + term
                    for t in range(8):
                        slot = ((t0 + t) // span) * span + ((t0 + t) % span ^ flip)
                        row = pl.multiple_of(slot * feeds + f0, 16)
                        value = jnp.concatenate([total[0][t], total[1][t]], axis=0)
                        filt[pl.ds(row, 16), p * CH + kk * LANES : p * CH + (kk + 1) * LANES] = (
                            value.astype(jnp.bfloat16)
                        )
        return carry

    lax.fori_loop(0, feeds // 16, strip, 0)

    for c in range(STEP * feeds // 256):
        product = lax.dot_general(
            tabs[...], filt[c * 256 : (c + 1) * 256, :], NT, preferred_element_type=jnp.float32
        )
        product = product.reshape(2 * CH // AVG, AVG, 256)
        packed = jnp.concatenate([product[:, :, :LANES], product[:, :, LANES:]], axis=1)
        packed = packed.astype(jnp.bfloat16).reshape(chans, outs_per_dev, 2, 2 * AVG, LANES)
        for k in range(chans):
            for g, (first, count) in enumerate(groups):
                outs[g * chans + k][:, :, c] = packed[k, first : first + count]


def channelize(voltages, me, window, table, first, steps, groups, chans):
    feeds = voltages.shape[1]
    outs_per_dev = CH // chans // AVG
    blocks = STEP * feeds // 256
    out_shape, out_specs = [], []
    for _, count in groups:
        for _ in range(chans):
            out_shape.append(
                jax.ShapeDtypeStruct((count, 2, steps * blocks, 2 * AVG, LANES), jnp.bfloat16)
            )
            out_specs.append(
                pl.BlockSpec((count, 2, blocks, 2 * AVG, LANES), lambda i, me: (0, 0, i, 0, 0))
            )
    block = (2, feeds, STEP * CH)
    rows = steps * STEP * feeds
    result = pl.pallas_call(
        functools.partial(channelize_kernel, (feeds, chans, outs_per_dev, groups)),
        grid_spec=pltpu.PrefetchScalarGridSpec(
            num_scalar_prefetch=1,
            grid=(steps,),
            in_specs=[
                pl.BlockSpec(block, lambda i, me: (0, 0, first + i)),
                pl.BlockSpec(block, lambda i, me: (0, 0, first + i + 1)),
                pl.BlockSpec((TAPS, 8, CH), lambda i, me: (0, 0, 0)),
                pl.BlockSpec((2 * CH, 2 * CH), lambda i, me: (0, 0)),
            ],
            out_specs=out_specs,
            scratch_shapes=[
                pltpu.VMEM((2 * CH, 2 * CH), jnp.bfloat16),
                pltpu.VMEM((STEP * feeds, 2 * CH), jnp.bfloat16),
            ],
        ),
        out_shape=out_shape,
        compiler_params=pltpu.CompilerParams(vmem_limit_bytes=VMEM),
        cost_estimate=pl.CostEstimate(
            flops=rows * (4 * CH * CH * 2 + 64 * CH * TAPS),
            bytes_accessed=steps * 2 * 2 * feeds * STEP * CH * 4 + rows * 4 * CH,
            transcendentals=0,
        ),
    )(me.reshape(1), voltages, voltages, window, table)
    return [result[g * chans : (g + 1) * chans] for g in range(len(groups))]


def correlate_kernel(sizes, feed_ref, *refs):
    feeds, chans, pieces, norm_scale = sizes
    own = refs[0 : 2 * pieces : 2]
    partner = refs[1 : 2 * pieces : 2]
    select = refs[2 * pieces]
    out_ref, rows_ref = refs[-2:]
    span = LANES // feeds
    inputs = select.shape[1]
    depth = rows_ref.shape[1] // 2

    @pl.when(pl.program_id(1) == 0)
    def _():
        low = lax.broadcasted_iota(jnp.int32, (256, LANES), 1) // feeds
        base = 0
        for piece in range(pieces):
            lines = own[piece].shape[3] * 16
            for x in range(span):
                for first in range(0, 2 * lines, 256):
                    tiles = []
                    for ref in (own[piece], partner[piece]):
                        for j in range(chans // span):
                            tile = None
                            for slot in range(span):
                                source = ref[j * span + (slot ^ x), 0].reshape(2 * lines, LANES)
                                source = source[first : first + 256]
                                tile = source if tile is None else jnp.where(low == slot, source, tile)
                            tiles.append(tile)
                    value = lax.dot_general(
                        select[x],
                        jnp.concatenate(tiles, axis=1),
                        NT,
                        preferred_element_type=jnp.float32,
                    ).astype(jnp.bfloat16)
                    start = first
                    while start < first + 256:
                        q, line = start // lines, start % lines
                        count = min(lines - line, first + 256 - start)
                        place = q * depth + base + line
                        rows_ref[:, place : place + count] = value[
                            :, start - first : start - first + count
                        ]
                        start += count
                base += lines

    half = out_ref.shape[2]
    mine = pl.ds(pl.multiple_of(feed_ref[0] * half, half), half)
    start = pl.multiple_of(pl.program_id(1) * COLS, COLS)
    other = pl.ds(start, COLS)

    def dot(left, right):
        return lax.dot_general(left, right, NT, preferred_element_type=jnp.float32)

    real, imag = slice(0, depth), slice(depth, 2 * depth)
    out_ref[0, 0] = dot(rows_ref[mine, :], rows_ref[other, :]) * norm_scale
    out_ref[1, 0] = (
        dot(rows_ref[mine, imag], rows_ref[other, real])
        - dot(rows_ref[mine, real], rows_ref[other, imag])
    ) * norm_scale


def correlate(feed, pieces, select, first, count, out_count, frames, feeds, chans, result):
    span, total, inputs = select.shape
    half = total // 2
    operands, in_specs = [], []
    depth = 0
    for own, partner, place in pieces:
        block = (chans, 1) + own.shape[2:]
        for array in (own, partner):
            operands.append(array)
            in_specs.append(
                pl.BlockSpec(
                    block,
                    functools.partial(lambda place, o, n, feed: (0, place + o, 0, 0, 0, 0), place),
                )
            )
        depth += own.shape[3] * 16 * span
    operands.append(select)
    in_specs.append(
        pl.BlockSpec(select.shape, lambda o, n, feed: (0, 0, 0), pipeline_mode=pl.Buffered(1))
    )
    aliases = {}
    if result is not None:
        aliases = {1 + len(operands): 0}
        operands.append(result)
        in_specs.append(pl.BlockSpec(memory_space=pl.ANY))
    return pl.pallas_call(
        functools.partial(correlate_kernel, (feeds, chans, len(pieces), 1.0 / (frames * AVG))),
        grid_spec=pltpu.PrefetchScalarGridSpec(
            num_scalar_prefetch=1,
            grid=(count, total // COLS),
            in_specs=in_specs,
            out_specs=pl.BlockSpec((2, 1, half, COLS), lambda o, n, feed: (0, first + o, 0, n)),
            scratch_shapes=[pltpu.VMEM((total, 2 * depth), jnp.bfloat16)],
        ),
        out_shape=jax.ShapeDtypeStruct((2, out_count, half, total), jnp.float32),
        input_output_aliases=aliases,
        compiler_params=pltpu.CompilerParams(vmem_limit_bytes=40 * 1024 * 1024),
        cost_estimate=pl.CostEstimate(flops=1000, bytes_accessed=1000, transcendentals=0),
    )(feed.reshape(1), *operands)


def body(voltages, input_order):
    feeds = voltages.shape[1]
    chans = lax.axis_size("chan")
    me = lax.axis_index("chan").astype(jnp.int32)
    feed = lax.axis_index("feed").astype(jnp.int32)
    frames = voltages.shape[2] // CH - TAPS + 1
    steps = frames // STEP
    outs_per_dev = CH // chans // AVG
    span = LANES // feeds
    window = jnp.asarray(make_window())
    table = jnp.asarray(make_table())

    k = jnp.arange(chans, dtype=jnp.int32)
    k = (k[None, :] // span) * span + ((k[None, :] % span) ^ jnp.arange(span, dtype=jnp.int32)[:, None])
    sources = (
        ((feed ^ jnp.arange(2, dtype=jnp.int32)) * (chans * feeds))[None, :, None, None]
        + ((me ^ k) * feeds)[:, None, :, None]
        + jnp.arange(feeds, dtype=jnp.int32)[None, None, None, :]
    ).reshape(span, 1, 2 * chans * feeds)
    select = (input_order[None, :, None] == sources).astype(jnp.bfloat16)

    near, far = range(1, chans // 2), range(chans // 2, chans)
    turns = [k for pair in zip(far, near) for k in pair] + [chans - 1]
    flying = []

    def send(blocks, order):
        received = {}
        for k in order:
            block = blocks[k]
            if len(flying) >= WINDOW:
                store, key = flying.pop(0)
                block, store[key] = lax.optimization_barrier((block, store[key]))
            received[k] = lax.ppermute(block, "chan", [(c, c ^ k) for c in range(chans)])
            flying.append((received, k))
        return received

    def share(block, received, result):
        if result is not None:
            received[1], result = lax.optimization_barrier((received[1], result))
        own = jnp.stack([block] + [received[k] for k in range(1, chans)])
        return (own, lax.ppermute(own, "feed", [(0, 1), (1, 0)])), result

    unit = LANES // feeds
    groups = [(0, outs_per_dev)]
    if outs_per_dev > 1:
        groups = [(0, outs_per_dev - 1), (outs_per_dev - 1, 1)]
    pieces = []
    if steps > unit:
        blocks = channelize(voltages, me, window, table, 0, unit, [(0, outs_per_dev)], chans)[0]
        blocks = list(blocks)
        pieces.append((blocks[0], send(blocks, turns)))
        me, blocks[0] = lax.optimization_barrier((me, blocks[0]))
        pieces[0] = (blocks[0], pieces[0][1])
        first = unit
    else:
        first = 0
    blocks = channelize(voltages, me, window, table, first, steps - first, groups, chans)
    sent = [send(group, turns) for group in blocks[:-1]]
    sent.append(send(blocks[-1], [*far, *near]))
    result = None
    shared = [share(block, received, None)[0] for block, received in pieces]
    for group, received, (first, count) in zip(blocks, sent, groups):
        block, result = share(group[0], received, result)
        result = correlate(
            feed, [piece + (first,) for piece in shared] + [block + (0,)],
            select, first, count, outs_per_dev, frames, feeds, chans, result,
        )
    return result


def solution(mesh):
    in_specs = (P(None, ("grp", "feed", "chan"), None), P())
    out_specs = P(None, ("grp", "chan"), "feed", None)
    return jax.shard_map(body, mesh=mesh, in_specs=in_specs, out_specs=out_specs, check_vma=False)
```

```python
import functools
import math

import jax
import jax.numpy as jnp
import numpy as np
from jax import lax
from jax.experimental import pallas as pl
from jax.experimental.pallas import tpu as pltpu
from jax.sharding import PartitionSpec as P

CH = 256
TAPS = 16
AVG = 8
LANES = 128
STEP = 16
COLS = 256
VMEM = 60 * 1024 * 1024
WINDOW = 5
NT = (((1,), (1,)), ((), ()))


def make_window():
    length = TAPS * CH
    position = np.arange(length, dtype=np.float64) + 0.5
    profile = np.sinc((position - length / 2) / CH) * (
        0.5 - 0.5 * np.cos(2 * math.pi * position / length)
    )
    profile = profile.astype(np.float32).reshape(TAPS, 1, CH) / np.float32(64 * math.sqrt(CH))
    return np.ascontiguousarray(np.broadcast_to(profile, (TAPS, 8, CH)))


def make_table():
    counter = np.arange(CH)
    angles = 2 * math.pi / CH * (counter[:, None] * counter[None, :] % CH)
    cosine, sine = np.cos(angles), np.sin(angles)
    table = np.stack(
        [np.concatenate([cosine, sine], axis=1), np.concatenate([-sine, cosine], axis=1)]
    )
    table = table.reshape(2, CH // AVG, AVG, 2 * CH).transpose(1, 0, 2, 3)
    return table.reshape(2 * CH, 2 * CH).astype(np.float32).astype(jnp.bfloat16)


def channelize_kernel(sizes, me_ref, va_ref, vb_ref, win_ref, tab_ref, *rest):
    feeds, chans, outs_per_dev, places = sizes
    outs, (tabs, filt) = rest[:-2], rest[-2:]
    me = me_ref[0]
    span = LANES // feeds
    part = 2 * AVG * outs_per_dev

    @pl.when(pl.program_id(0) == 0)
    def _():
        for k in range(chans):
            start = pl.multiple_of((me ^ k) * part, part)
            tabs[k * part : (k + 1) * part, :] = tab_ref[pl.ds(start, part), :]

    flip = lax.rem(me, span)

    def strip(index, carry):
        f0 = pl.multiple_of(index * 16, 16)
        for p in range(2):
            for kk in range(CH // LANES):
                lanes = slice(kk * LANES, (kk + 1) * LANES)
                weights = [win_ref[tap, :, lanes] for tap in range(TAPS)]
                for t0 in range(0, STEP, 8):
                    total = [[None] * 8, [None] * 8]
                    for u in range(t0, t0 + 8 + TAPS - 1):
                        src = va_ref if u < STEP else vb_ref
                        col = (u % STEP) * CH + kk * LANES
                        both = src[p, pl.ds(f0, 16), col : col + LANES].astype(jnp.float32)
                        for half in range(2):
                            x = both[half * 8 : half * 8 + 8]
                            for t in range(8):
                                tap = u - t0 - t
                                if 0 <= tap < TAPS:
                                    term = weights[tap] * x
                                    old = total[half][t]
                                    total[half][t] = term if old is None else old + term
                    for t in range(8):
                        slot = ((t0 + t) // span) * span + ((t0 + t) % span ^ flip)
                        row = pl.multiple_of(slot * feeds + f0, 16)
                        value = jnp.concatenate([total[0][t], total[1][t]], axis=0)
                        filt[pl.ds(row, 16), p * CH + kk * LANES : p * CH + (kk + 1) * LANES] = (
                            value.astype(jnp.bfloat16)
                        )
        return carry

    lax.fori_loop(0, feeds // 16, strip, 0)

    for c in range(STEP * feeds // 256):
        product = lax.dot_general(
            tabs[...], filt[c * 256 : (c + 1) * 256, :], NT, preferred_element_type=jnp.float32
        )
        product = product.reshape(2 * CH // AVG, AVG, 256)
        packed = jnp.concatenate([product[:, :, :LANES], product[:, :, LANES:]], axis=1)
        packed = packed.astype(jnp.bfloat16).reshape(chans, outs_per_dev, 2, 2 * AVG, LANES)
        for out, (k, first, count) in zip(outs, places):
            out[:, :, c] = packed[k, first : first + count]


def channelize(voltages, me, window, table, first, steps, groups, chans):
    feeds = voltages.shape[1]
    outs_per_dev = CH // chans // AVG
    blocks = STEP * feeds // 256
    out_shape, out_specs = [], []
    places = [(k, 0, outs_per_dev) for k in range(chans // 2)]
    places += [(k, begin, count) for begin, count in groups for k in range(chans // 2, chans)]
    for _, _, count in places:
        out_shape.append(
            jax.ShapeDtypeStruct((count, 2, steps * blocks, 2 * AVG, LANES), jnp.bfloat16)
        )
        out_specs.append(
            pl.BlockSpec((count, 2, blocks, 2 * AVG, LANES), lambda i, me: (0, 0, i, 0, 0))
        )
    block = (2, feeds, STEP * CH)
    rows = steps * STEP * feeds
    result = pl.pallas_call(
        functools.partial(channelize_kernel, (feeds, chans, outs_per_dev, places)),
        grid_spec=pltpu.PrefetchScalarGridSpec(
            num_scalar_prefetch=1,
            grid=(steps,),
            in_specs=[
                pl.BlockSpec(block, lambda i, me: (0, 0, first + i)),
                pl.BlockSpec(block, lambda i, me: (0, 0, first + i + 1)),
                pl.BlockSpec((TAPS, 8, CH), lambda i, me: (0, 0, 0)),
                pl.BlockSpec((2 * CH, 2 * CH), lambda i, me: (0, 0)),
            ],
            out_specs=out_specs,
            scratch_shapes=[
                pltpu.VMEM((2 * CH, 2 * CH), jnp.bfloat16),
                pltpu.VMEM((STEP * feeds, 2 * CH), jnp.bfloat16),
            ],
        ),
        out_shape=out_shape,
        compiler_params=pltpu.CompilerParams(vmem_limit_bytes=VMEM),
        cost_estimate=pl.CostEstimate(
            flops=rows * (4 * CH * CH * 2 + 64 * CH * TAPS),
            bytes_accessed=steps * 2 * 2 * feeds * STEP * CH * 4 + rows * 4 * CH,
            transcendentals=0,
        ),
    )(me.reshape(1), voltages, voltages, window, table)
    half = chans // 2
    near = list(result[:half])
    far = [
        dict(zip(range(half, chans), result[half * (g + 1) : half * (g + 2)]))
        for g in range(len(groups))
    ]
    return far, near


def correlate_kernel(sizes, feed_ref, *refs):
    feeds, chans, pieces, norm_scale, adds = sizes
    own = refs[0 : 2 * pieces : 2]
    partner = refs[1 : 2 * pieces : 2]
    select = refs[2 * pieces]
    out_ref, rows_ref = refs[-2:]
    span = LANES // feeds
    inputs = select.shape[1]
    depth = rows_ref.shape[1] // 2

    @pl.when(pl.program_id(1) == 0)
    def _():
        low = lax.broadcasted_iota(jnp.int32, (256, LANES), 1) // feeds
        base = 0
        for piece in range(pieces):
            lines = own[piece].shape[3] * 16
            for x in range(span):
                for first in range(0, 2 * lines, 256):
                    tiles = []
                    for ref in (own[piece], partner[piece]):
                        for j in range(chans // span):
                            tile = None
                            for slot in range(span):
                                source = ref[j * span + (slot ^ x), 0].reshape(2 * lines, LANES)
                                source = source[first : first + 256]
                                tile = source if tile is None else jnp.where(low == slot, source, tile)
                            tiles.append(tile)
                    value = lax.dot_general(
                        select[x],
                        jnp.concatenate(tiles, axis=1),
                        NT,
                        preferred_element_type=jnp.float32,
                    ).astype(jnp.bfloat16)
                    start = first
                    while start < first + 256:
                        q, line = start // lines, start % lines
                        count = min(lines - line, first + 256 - start)
                        place = q * depth + base + line
                        rows_ref[:, place : place + count] = value[
                            :, start - first : start - first + count
                        ]
                        start += count
                base += lines

    half = out_ref.shape[2]
    mine = pl.ds(pl.multiple_of(feed_ref[0] * half, half), half)
    start = pl.multiple_of(pl.program_id(1) * COLS, COLS)
    other = pl.ds(start, COLS)

    def dot(left, right):
        return lax.dot_general(left, right, NT, preferred_element_type=jnp.float32)

    real, imag = slice(0, depth), slice(depth, 2 * depth)
    out_re = dot(rows_ref[mine, :], rows_ref[other, :]) * norm_scale
    out_im = (
        dot(rows_ref[mine, imag], rows_ref[other, real])
        - dot(rows_ref[mine, real], rows_ref[other, imag])
    ) * norm_scale
    if adds:
        before = refs[2 * pieces + 1]
        out_re = out_re + before[0, 0]
        out_im = out_im + before[1, 0]
    out_ref[0, 0] = out_re
    out_ref[1, 0] = out_im


def correlate(feed, pieces, select, first, count, out_count, frames, feeds, chans, result, adds):
    span, total, inputs = select.shape
    half = total // 2
    operands, in_specs = [], []
    depth = 0
    for own, partner, place in pieces:
        block = (chans, 1) + own.shape[2:]
        for array in (own, partner):
            operands.append(array)
            in_specs.append(
                pl.BlockSpec(
                    block,
                    functools.partial(lambda place, o, n, feed: (0, place + o, 0, 0, 0, 0), place),
                )
            )
        depth += own.shape[3] * 16 * span
    operands.append(select)
    in_specs.append(
        pl.BlockSpec(select.shape, lambda o, n, feed: (0, 0, 0), pipeline_mode=pl.Buffered(1))
    )
    out_spec = pl.BlockSpec((2, 1, half, COLS), lambda o, n, feed: (0, first + o, 0, n))
    aliases = {}
    if result is not None:
        aliases = {1 + len(operands): 0}
        operands.append(result)
        in_specs.append(out_spec if adds else pl.BlockSpec(memory_space=pl.ANY))
    return pl.pallas_call(
        functools.partial(
            correlate_kernel, (feeds, chans, len(pieces), 1.0 / (frames * AVG), adds)
        ),
        grid_spec=pltpu.PrefetchScalarGridSpec(
            num_scalar_prefetch=1,
            grid=(count, total // COLS),
            in_specs=in_specs,
            out_specs=out_spec,
            scratch_shapes=[pltpu.VMEM((total, 2 * depth), jnp.bfloat16)],
        ),
        out_shape=jax.ShapeDtypeStruct((2, out_count, half, total), jnp.float32),
        input_output_aliases=aliases,
        compiler_params=pltpu.CompilerParams(vmem_limit_bytes=40 * 1024 * 1024),
        cost_estimate=pl.CostEstimate(flops=1000, bytes_accessed=1000, transcendentals=0),
    )(feed.reshape(1), *operands)


def body(voltages, input_order):
    feeds = voltages.shape[1]
    chans = lax.axis_size("chan")
    me = lax.axis_index("chan").astype(jnp.int32)
    feed = lax.axis_index("feed").astype(jnp.int32)
    frames = voltages.shape[2] // CH - TAPS + 1
    steps = frames // STEP
    outs_per_dev = CH // chans // AVG
    span = LANES // feeds
    window = jnp.asarray(make_window())
    table = jnp.asarray(make_table())

    k = jnp.arange(chans, dtype=jnp.int32)
    k = (k[None, :] // span) * span + ((k[None, :] % span) ^ jnp.arange(span, dtype=jnp.int32)[:, None])
    sources = (
        ((feed ^ jnp.arange(2, dtype=jnp.int32)) * (chans * feeds))[None, :, None, None]
        + ((me ^ k) * feeds)[:, None, :, None]
        + jnp.arange(feeds, dtype=jnp.int32)[None, None, None, :]
    ).reshape(span, 1, 2 * chans * feeds)
    select = (input_order[None, :, None] == sources).astype(jnp.bfloat16)

    near, far = list(range(1, chans // 2)), list(range(chans // 2, chans))
    turns = [k for pair in zip(far, near) for k in pair] + far[-1:]
    flying = []

    def send(k, block, *after):
        if len(flying) >= WINDOW:
            store, key = flying.pop(0)
            block, store[key] = lax.optimization_barrier((block, store[key]))
        if after:
            block, *after = lax.optimization_barrier((block, *after))
        store = {k: lax.ppermute(block, "chan", [(c, c ^ k) for c in range(chans)])}
        flying.append((store, k))
        return store

    def share(block, received, begin=0, count=None):
        parts = [block]
        for k in range(1, chans):
            array = received[k][k]
            parts.append(array if count is None or array.shape[0] == count else array[begin : begin + count])
        own = jnp.stack(parts)
        return own, lax.ppermute(own, "feed", [(0, 1), (1, 0)])

    unit = LANES // feeds
    first = unit if steps > unit else 0
    groups = [(0, outs_per_dev)]
    if outs_per_dev > 1:
        groups = [(0, outs_per_dev - 1), (outs_per_dev - 1, 1)]
    if first:
        start_far, start = channelize(
            voltages, me, window, table, 0, first, [(0, outs_per_dev)], chans
        )
        start_far[0].update({k: start[k] for k in near})
        me, start[0] = lax.optimization_barrier((me, start[0]))
    far_blocks, near_blocks = channelize(
        voltages, me, window, table, first, steps - first, groups, chans
    )
    result = early = None
    if first:
        early = {}
        for place, k in enumerate(turns):
            block = start_far[0][k]
            if place == WINDOW:
                block, near_blocks[0] = lax.optimization_barrier((block, near_blocks[0]))
            early[k] = send(k, block)
    sent = [{k: None for k in near} for _ in groups]
    for place, k in enumerate(turns):
        block = near_blocks[k] if k in near else far_blocks[0][k]
        if first and place == len(turns) - 2:
            own, partner = share(start[0], early)
            result = correlate(
                feed, [(own, partner, 0)],
                select, 0, outs_per_dev, outs_per_dev, frames, feeds, chans, None, False,
            )
            block, result = lax.optimization_barrier((block, result))
        store = send(k, block)
        for received in sent if k in near else sent[:1]:
            received[k] = store
    for k in far if len(groups) > 1 else []:
        sent[1][k] = send(k, far_blocks[1][k])
    for g, (begin, count) in enumerate(groups):
        mine = near_blocks[0][begin : begin + count]
        if g:
            mine, result = lax.optimization_barrier((mine, result))
        result = correlate(
            feed, [share(mine, sent[g], begin, count) + (0,)],
            select, begin, count, outs_per_dev, frames, feeds, chans, result, first > 0,
        )
    return result


def solution(mesh):
    in_specs = (P(None, ("grp", "feed", "chan"), None), P())
    out_specs = P(None, ("grp", "chan"), "feed", None)
    return jax.shard_map(body, mesh=mesh, in_specs=in_specs, out_specs=out_specs, check_vma=False)
```

```python
import functools
import math

import jax
import jax.numpy as jnp
import numpy as np
from jax import lax
from jax.experimental import pallas as pl
from jax.experimental.pallas import tpu as pltpu
from jax.sharding import PartitionSpec as P

CH = 256
TAPS = 16
AVG = 8
LANES = 128
STEP = 16
COLS = 512
VMEM = 60 * 1024 * 1024
WINDOW = 5
NT = (((1,), (1,)), ((), ()))


def make_window():
    length = TAPS * CH
    position = np.arange(length, dtype=np.float64) + 0.5
    profile = np.sinc((position - length / 2) / CH) * (
        0.5 - 0.5 * np.cos(2 * math.pi * position / length)
    )
    profile = profile.astype(np.float32).reshape(TAPS, 1, CH) / np.float32(64 * math.sqrt(CH))
    return np.ascontiguousarray(np.broadcast_to(profile, (TAPS, 8, CH)))


def make_table():
    counter = np.arange(CH)
    angles = 2 * math.pi / CH * (counter[:, None] * counter[None, :] % CH)
    cosine, sine = np.cos(angles), np.sin(angles)
    table = np.stack(
        [np.concatenate([cosine, sine], axis=1), np.concatenate([-sine, cosine], axis=1)]
    )
    table = table.reshape(2, CH // AVG, AVG, 2 * CH).transpose(1, 0, 2, 3)
    return table.reshape(2 * CH, 2 * CH).astype(np.float32).astype(jnp.bfloat16)


def channelize_kernel(sizes, me_ref, va_ref, vb_ref, win_ref, tab_ref, *rest):
    feeds, chans, outs_per_dev, places = sizes
    outs, (tabs, filt) = rest[:-2], rest[-2:]
    me = me_ref[0]
    span = LANES // feeds
    part = 2 * AVG * outs_per_dev

    @pl.when(pl.program_id(0) == 0)
    def _():
        for k in range(chans):
            start = pl.multiple_of((me ^ k) * part, part)
            tabs[k * part : (k + 1) * part, :] = tab_ref[pl.ds(start, part), :]

    flip = lax.rem(me, span)

    def strip(index, carry):
        f0 = pl.multiple_of(index * 16, 16)
        for p in range(2):
            for kk in range(CH // LANES):
                lanes = slice(kk * LANES, (kk + 1) * LANES)
                weights = [win_ref[tap, :, lanes] for tap in range(TAPS)]
                for t0 in range(0, STEP, 8):
                    total = [[None] * 8, [None] * 8]
                    for u in range(t0, t0 + 8 + TAPS - 1):
                        src = va_ref if u < STEP else vb_ref
                        col = (u % STEP) * CH + kk * LANES
                        both = src[p, pl.ds(f0, 16), col : col + LANES].astype(jnp.float32)
                        for half in range(2):
                            x = both[half * 8 : half * 8 + 8]
                            for t in range(8):
                                tap = u - t0 - t
                                if 0 <= tap < TAPS:
                                    term = weights[tap] * x
                                    old = total[half][t]
                                    total[half][t] = term if old is None else old + term
                    for t in range(8):
                        slot = ((t0 + t) // span) * span + ((t0 + t) % span ^ flip)
                        row = pl.multiple_of(slot * feeds + f0, 16)
                        value = jnp.concatenate([total[0][t], total[1][t]], axis=0)
                        filt[pl.ds(row, 16), p * CH + kk * LANES : p * CH + (kk + 1) * LANES] = (
                            value.astype(jnp.bfloat16)
                        )
        return carry

    lax.fori_loop(0, feeds // 16, strip, 0)

    for c in range(STEP * feeds // 256):
        product = lax.dot_general(
            tabs[...], filt[c * 256 : (c + 1) * 256, :], NT, preferred_element_type=jnp.float32
        )
        product = product.reshape(2 * CH // AVG, AVG, 256)
        packed = jnp.concatenate([product[:, :, :LANES], product[:, :, LANES:]], axis=1)
        packed = packed.astype(jnp.bfloat16).reshape(chans, outs_per_dev, 2, 2 * AVG, LANES)
        for out, (k, first, count) in zip(outs, places):
            out[:, :, c] = packed[k, first : first + count]


def channelize(voltages, me, window, table, first, steps, groups, chans):
    feeds = voltages.shape[1]
    outs_per_dev = CH // chans // AVG
    blocks = STEP * feeds // 256
    out_shape, out_specs = [], []
    places = [(k, 0, outs_per_dev) for k in range(chans // 2)]
    places += [(k, begin, count) for begin, count in groups for k in range(chans // 2, chans)]
    for _, _, count in places:
        out_shape.append(
            jax.ShapeDtypeStruct((count, 2, steps * blocks, 2 * AVG, LANES), jnp.bfloat16)
        )
        out_specs.append(
            pl.BlockSpec((count, 2, blocks, 2 * AVG, LANES), lambda i, me: (0, 0, i, 0, 0))
        )
    block = (2, feeds, STEP * CH)
    rows = steps * STEP * feeds
    result = pl.pallas_call(
        functools.partial(channelize_kernel, (feeds, chans, outs_per_dev, places)),
        grid_spec=pltpu.PrefetchScalarGridSpec(
            num_scalar_prefetch=1,
            grid=(steps,),
            in_specs=[
                pl.BlockSpec(block, lambda i, me: (0, 0, first + i)),
                pl.BlockSpec(block, lambda i, me: (0, 0, first + i + 1)),
                pl.BlockSpec((TAPS, 8, CH), lambda i, me: (0, 0, 0)),
                pl.BlockSpec((2 * CH, 2 * CH), lambda i, me: (0, 0)),
            ],
            out_specs=out_specs,
            scratch_shapes=[
                pltpu.VMEM((2 * CH, 2 * CH), jnp.bfloat16),
                pltpu.VMEM((STEP * feeds, 2 * CH), jnp.bfloat16),
            ],
        ),
        out_shape=out_shape,
        compiler_params=pltpu.CompilerParams(vmem_limit_bytes=VMEM),
        cost_estimate=pl.CostEstimate(
            flops=rows * (4 * CH * CH * 2 + 64 * CH * TAPS),
            bytes_accessed=steps * 2 * 2 * feeds * STEP * CH * 4 + rows * 4 * CH,
            transcendentals=0,
        ),
    )(me.reshape(1), voltages, voltages, window, table)
    half = chans // 2
    near = list(result[:half])
    far = [
        dict(zip(range(half, chans), result[half * (g + 1) : half * (g + 2)]))
        for g in range(len(groups))
    ]
    return far, near


def correlate_kernel(sizes, feed_ref, *refs):
    feeds, pieces, norm_scale, adds, copies, begin = sizes
    own = [(ref, k) for ref in refs[0 : 2 * pieces : 2] for k in range(ref.shape[0])]
    partner = [(ref, k) for ref in refs[1 : 2 * pieces : 2] for k in range(ref.shape[0])]
    select = refs[2 * pieces]
    if copies:
        out_ref, rows_ref, before_ref, sem = refs[-4:]
        before = pltpu.make_async_copy(
            refs[2 * pieces + 1].at[:, begin + pl.program_id(0)], before_ref, sem
        )
    else:
        out_ref, rows_ref = refs[-2:]
    span = LANES // feeds
    depth = rows_ref.shape[1] // 2
    lines = depth // span

    @pl.when(pl.program_id(1) == 0)
    def _():
        if copies:
            before.start()
        lane_slot = lax.broadcasted_iota(jnp.int32, (256, LANES), 1) // feeds
        for x in range(span):
            for first in range(0, 2 * lines, 256):
                tiles = []
                for blocks in (own, partner):
                    for j in range(0, len(blocks), span):
                        tile = None
                        for slot in range(span):
                            ref, k = blocks[j + (slot ^ x)]
                            source = ref[k, 0].reshape(2 * lines, LANES)[first : first + 256]
                            if tile is None:
                                tile = source
                            else:
                                tile = jnp.where(lane_slot == slot, source, tile)
                        for bit in (1 << n for n in range(x.bit_length()) if x >> n & 1):
                            shift = bit * feeds
                            left = pltpu.roll(tile, LANES - shift, 1)
                            right = pltpu.roll(tile, shift, 1)
                            tile = jnp.where((lane_slot & bit) == 0, left, right)
                        tiles.append(tile)
                value = lax.dot_general(
                    select[...], jnp.concatenate(tiles, axis=1), NT, preferred_element_type=jnp.float32
                ).astype(jnp.bfloat16)
                start = first
                while start < first + 256:
                    q, line = start // lines, start % lines
                    count = min(lines - line, first + 256 - start)
                    place = q * depth + x * lines + line
                    rows_ref[:, place : place + count] = value[
                        :, start - first : start - first + count
                    ]
                    start += count

        if copies:
            before.wait()

    half = out_ref.shape[2]
    mine = pl.ds(pl.multiple_of(feed_ref[0] * half, half), half)
    start = pl.multiple_of(pl.program_id(1) * COLS, COLS)
    other = pl.ds(start, COLS)

    def dot(left, right):
        return lax.dot_general(left, right, NT, preferred_element_type=jnp.float32)

    real, imag = slice(0, depth), slice(depth, 2 * depth)
    out_re = dot(rows_ref[mine, :], rows_ref[other, :]) * norm_scale
    out_im = (
        dot(rows_ref[mine, imag], rows_ref[other, real])
        - dot(rows_ref[mine, real], rows_ref[other, imag])
    ) * norm_scale
    if copies:
        out_re = out_re + before_ref[0, :, other]
        out_im = out_im + before_ref[1, :, other]
    elif adds:
        out_re = out_re + refs[2 * pieces + 1][0, 0]
        out_im = out_im + refs[2 * pieces + 1][1, 0]
    out_ref[0, 0] = out_re
    out_ref[1, 0] = out_im


def correlate(feed, pieces, select, first, count, out_count, frames, feeds, result, adds):
    span = LANES // feeds
    total = select.shape[0]
    half = total // 2
    operands, in_specs = [], []
    for pair in pieces:
        for array in pair:
            operands.append(array)
            in_specs.append(
                pl.BlockSpec(
                    (array.shape[0], 1) + array.shape[2:], lambda o, n, feed: (0, o, 0, 0, 0, 0)
                )
            )
    depth = array.shape[3] * 16 * span
    operands.append(select)
    in_specs.append(
        pl.BlockSpec(select.shape, lambda o, n, feed: (0, 0), pipeline_mode=pl.Buffered(1))
    )
    out_spec = pl.BlockSpec((2, 1, half, COLS), lambda o, n, feed: (0, first + o, 0, n))
    copies = adds and count == 1
    aliases = {}
    if result is not None:
        aliases = {1 + len(operands): 0}
        operands.append(result)
        in_specs.append(out_spec if adds and not copies else pl.BlockSpec(memory_space=pl.ANY))
    scratch = [pltpu.VMEM((total, 2 * depth), jnp.bfloat16)]
    if copies:
        scratch += [pltpu.VMEM((2, half, total), jnp.float32), pltpu.SemaphoreType.DMA]
    return pl.pallas_call(
        functools.partial(
            correlate_kernel, (feeds, len(pieces), 1.0 / (frames * AVG), adds, copies, first)
        ),
        grid_spec=pltpu.PrefetchScalarGridSpec(
            num_scalar_prefetch=1,
            grid=(count, total // COLS),
            in_specs=in_specs,
            out_specs=out_spec,
            scratch_shapes=scratch,
        ),
        out_shape=jax.ShapeDtypeStruct((2, out_count, half, total), jnp.float32),
        input_output_aliases=aliases,
        compiler_params=pltpu.CompilerParams(vmem_limit_bytes=40 * 1024 * 1024),
        cost_estimate=pl.CostEstimate(flops=1000, bytes_accessed=1000, transcendentals=0),
    )(feed.reshape(1), *operands)


def body(voltages, input_order):
    feeds = voltages.shape[1]
    chans = lax.axis_size("chan")
    me = lax.axis_index("chan").astype(jnp.int32)
    feed = lax.axis_index("feed").astype(jnp.int32)
    frames = voltages.shape[2] // CH - TAPS + 1
    steps = frames // STEP
    outs_per_dev = CH // chans // AVG
    window = jnp.asarray(make_window())
    table = jnp.asarray(make_table())

    sources = (
        ((feed ^ jnp.arange(2, dtype=jnp.int32)) * (chans * feeds))[:, None, None]
        + ((me ^ jnp.arange(chans, dtype=jnp.int32)) * feeds)[None, :, None]
        + jnp.arange(feeds, dtype=jnp.int32)[None, None, :]
    ).reshape(1, 2 * chans * feeds)
    select = (input_order[:, None] == sources).astype(jnp.bfloat16)

    near, far = list(range(1, chans // 2)), list(range(chans // 2, chans))
    turns = [k for pair in zip(far, near) for k in pair] + far[-1:]
    flying = []

    def send(k, block, *after):
        if len(flying) >= WINDOW:
            store, key = flying.pop(0)
            block, store[key] = lax.optimization_barrier((block, store[key]))
        if after:
            block, *after = lax.optimization_barrier((block, *after))
        store = {k: lax.ppermute(block, "chan", [(c, c ^ k) for c in range(chans)])}
        flying.append((store, k))
        return store

    def share(block, received, cuts, begin=0, count=None):
        parts = [block]
        for k in range(1, chans):
            array = received[k][k]
            whole = count is None or array.shape[0] == count
            parts.append(array if whole else array[begin : begin + count])
        pieces = []
        for low, high in zip([0] + cuts, cuts):
            own = jnp.stack(parts[low:high])
            pieces.append((own, lax.ppermute(own, "feed", [(0, 1), (1, 0)])))
        return pieces

    unit = LANES // feeds
    first = unit if steps > unit else 0
    groups = [(0, outs_per_dev)]
    if outs_per_dev > 1:
        groups = [(0, outs_per_dev - 1), (outs_per_dev - 1, 1)]
    if first:
        start_far, start = channelize(
            voltages, me, window, table, 0, first, [(0, outs_per_dev)], chans
        )
        start_far[0].update({k: start[k] for k in near})
        me, start[0] = lax.optimization_barrier((me, start[0]))
    far_blocks, near_blocks = channelize(
        voltages, me, window, table, first, steps - first, groups, chans
    )
    result = early = None
    if first:
        early = {}
        for place, k in enumerate(turns):
            block = start_far[0][k]
            if place == WINDOW:
                block, near_blocks[0] = lax.optimization_barrier((block, near_blocks[0]))
            early[k] = send(k, block)
    sent = [{k: None for k in near} for _ in groups]
    for place, k in enumerate(turns):
        block = near_blocks[k] if k in near else far_blocks[0][k]
        if first and place == len(turns) - 2:
            result = correlate(
                feed, share(start[0], early, [chans]),
                select, 0, outs_per_dev, outs_per_dev, frames, feeds, None, False,
            )
            block, result = lax.optimization_barrier((block, result))
        store = send(k, block)
        for received in sent if k in near else sent[:1]:
            received[k] = store
    for k in far if len(groups) > 1 else []:
        sent[1][k] = send(k, far_blocks[1][k])
    for g, (begin, count) in enumerate(groups):
        mine = near_blocks[0][begin : begin + count]
        if g:
            mine, result = lax.optimization_barrier((mine, result))
        result = correlate(
            feed, share(mine, sent[g], [chans], begin, count),
            select, begin, count, outs_per_dev, frames, feeds, result, first > 0,
        )
    return result


def solution(mesh):
    in_specs = (P(None, ("grp", "feed", "chan"), None), P())
    out_specs = P(None, ("grp", "chan"), "feed", None)
    return jax.shard_map(body, mesh=mesh, in_specs=in_specs, out_specs=out_specs, check_vma=False)
```

```python
import functools
import math

import jax
import jax.numpy as jnp
import numpy as np
from jax import lax
from jax.experimental import pallas as pl
from jax.experimental.pallas import tpu as pltpu
from jax.sharding import PartitionSpec as P

CH = 256
TAPS = 16
AVG = 8
LANES = 128
STEP = 16
COLS = 512
VMEM = 60 * 1024 * 1024
WINDOW = 5
NT = (((1,), (1,)), ((), ()))


def make_window():
    length = TAPS * CH
    position = np.arange(length, dtype=np.float64) + 0.5
    profile = np.sinc((position - length / 2) / CH) * (
        0.5 - 0.5 * np.cos(2 * math.pi * position / length)
    )
    profile = profile.astype(np.float32).reshape(TAPS, 1, CH) / np.float32(64 * math.sqrt(CH))
    return np.ascontiguousarray(np.broadcast_to(profile, (TAPS, 8, CH)))


def make_table():
    counter = np.arange(CH)
    angles = 2 * math.pi / CH * (counter[:, None] * counter[None, :] % CH)
    cosine, sine = np.cos(angles), np.sin(angles)
    table = np.stack(
        [np.concatenate([cosine, sine], axis=1), np.concatenate([-sine, cosine], axis=1)]
    )
    table = table.reshape(2, CH // AVG, AVG, 2 * CH).transpose(1, 0, 2, 3)
    return table.reshape(2 * CH, 2 * CH).astype(np.float32).astype(jnp.bfloat16)


def channelize_kernel(sizes, me_ref, va_ref, vb_ref, win_ref, tab_ref, *rest):
    feeds, chans, outs_per_dev, places = sizes
    outs, (tabs, filt) = rest[:-2], rest[-2:]
    me = me_ref[0]
    span = LANES // feeds
    part = 2 * AVG * outs_per_dev

    @pl.when(pl.program_id(0) == 0)
    def _():
        for k in range(chans):
            start = pl.multiple_of((me ^ k) * part, part)
            tabs[k * part : (k + 1) * part, :] = tab_ref[pl.ds(start, part), :]

    flip = lax.rem(me, span)

    def strip(index, carry):
        f0 = pl.multiple_of(index * 16, 16)
        for p in range(2):
            for kk in range(CH // LANES):
                lanes = slice(kk * LANES, (kk + 1) * LANES)
                weights = [win_ref[tap, :, lanes] for tap in range(TAPS)]
                for t0 in range(0, STEP, 8):
                    total = [[None] * 8, [None] * 8]
                    for u in range(t0, t0 + 8 + TAPS - 1):
                        src = va_ref if u < STEP else vb_ref
                        col = (u % STEP) * CH + kk * LANES
                        both = src[p, pl.ds(f0, 16), col : col + LANES].astype(jnp.float32)
                        for half in range(2):
                            x = both[half * 8 : half * 8 + 8]
                            for t in range(8):
                                tap = u - t0 - t
                                if 0 <= tap < TAPS:
                                    term = weights[tap] * x
                                    old = total[half][t]
                                    total[half][t] = term if old is None else old + term
                    for t in range(8):
                        slot = ((t0 + t) // span) * span + ((t0 + t) % span ^ flip)
                        row = pl.multiple_of(slot * feeds + f0, 16)
                        value = jnp.concatenate([total[0][t], total[1][t]], axis=0)
                        filt[pl.ds(row, 16), p * CH + kk * LANES : p * CH + (kk + 1) * LANES] = (
                            value.astype(jnp.bfloat16)
                        )
        return carry

    lax.fori_loop(0, feeds // 16, strip, 0)

    for c in range(STEP * feeds // 256):
        product = lax.dot_general(
            tabs[...], filt[c * 256 : (c + 1) * 256, :], NT, preferred_element_type=jnp.float32
        )
        product = product.reshape(2 * CH // AVG, AVG, 256)
        packed = jnp.concatenate([product[:, :, :LANES], product[:, :, LANES:]], axis=1)
        packed = packed.astype(jnp.bfloat16).reshape(chans, outs_per_dev, 2, 2 * AVG, LANES)
        for out, (k, first, count) in zip(outs, places):
            out[:, :, c] = packed[k, first : first + count]


def channelize(voltages, me, window, table, first, steps, groups, chans):
    feeds = voltages.shape[1]
    outs_per_dev = CH // chans // AVG
    blocks = STEP * feeds // 256
    out_shape, out_specs = [], []
    places = [(k, 0, outs_per_dev) for k in range(chans // 2)]
    places += [(k, begin, count) for begin, count in groups for k in range(chans // 2, chans)]
    for _, _, count in places:
        out_shape.append(
            jax.ShapeDtypeStruct((count, 2, steps * blocks, 2 * AVG, LANES), jnp.bfloat16)
        )
        out_specs.append(
            pl.BlockSpec((count, 2, blocks, 2 * AVG, LANES), lambda i, me: (0, 0, i, 0, 0))
        )
    block = (2, feeds, STEP * CH)
    rows = steps * STEP * feeds
    result = pl.pallas_call(
        functools.partial(channelize_kernel, (feeds, chans, outs_per_dev, places)),
        grid_spec=pltpu.PrefetchScalarGridSpec(
            num_scalar_prefetch=1,
            grid=(steps,),
            in_specs=[
                pl.BlockSpec(block, lambda i, me: (0, 0, first + i)),
                pl.BlockSpec(block, lambda i, me: (0, 0, first + i + 1)),
                pl.BlockSpec((TAPS, 8, CH), lambda i, me: (0, 0, 0)),
                pl.BlockSpec((2 * CH, 2 * CH), lambda i, me: (0, 0)),
            ],
            out_specs=out_specs,
            scratch_shapes=[
                pltpu.VMEM((2 * CH, 2 * CH), jnp.bfloat16),
                pltpu.VMEM((STEP * feeds, 2 * CH), jnp.bfloat16),
            ],
        ),
        out_shape=out_shape,
        compiler_params=pltpu.CompilerParams(vmem_limit_bytes=VMEM),
        cost_estimate=pl.CostEstimate(
            flops=rows * (4 * CH * CH * 2 + 64 * CH * TAPS),
            bytes_accessed=steps * 2 * 2 * feeds * STEP * CH * 4 + rows * 4 * CH,
            transcendentals=0,
        ),
    )(me.reshape(1), voltages, voltages, window, table)
    half = chans // 2
    near = list(result[:half])
    far = [
        dict(zip(range(half, chans), result[half * (g + 1) : half * (g + 2)]))
        for g in range(len(groups))
    ]
    return far, near


def correlate_kernel(sizes, feed_ref, *refs):
    feeds, pieces, norm_scale, adds, copies, begin = sizes
    own = [(ref, k) for ref in refs[0 : 2 * pieces : 2] for k in range(ref.shape[0])]
    partner = [(ref, k) for ref in refs[1 : 2 * pieces : 2] for k in range(ref.shape[0])]
    select = refs[2 * pieces]
    if copies:
        out_ref, rows_ref, before_ref, sem = refs[-4:]
        before = pltpu.make_async_copy(
            refs[2 * pieces + 1].at[:, begin + pl.program_id(0)], before_ref, sem
        )
    else:
        out_ref, rows_ref = refs[-2:]
    span = LANES // feeds
    depth = rows_ref.shape[1] // 2
    lines = depth // span

    @pl.when(pl.program_id(1) == 0)
    def _():
        if copies:
            before.start()
        lane_slot = lax.broadcasted_iota(jnp.int32, (256, LANES), 1) // feeds
        for x in range(span):
            for first in range(0, 2 * lines, 256):
                tiles = []
                for blocks in (own, partner):
                    for j in range(0, len(blocks), span):
                        tile = None
                        for slot in range(span):
                            ref, k = blocks[j + (slot ^ x)]
                            source = ref[k, 0].reshape(2 * lines, LANES)[first : first + 256]
                            if tile is None:
                                tile = source
                            else:
                                tile = jnp.where(lane_slot == slot, source, tile)
                        for bit in (1 << n for n in range(x.bit_length()) if x >> n & 1):
                            shift = bit * feeds
                            left = pltpu.roll(tile, LANES - shift, 1)
                            right = pltpu.roll(tile, shift, 1)
                            tile = jnp.where((lane_slot & bit) == 0, left, right)
                        tiles.append(tile)
                value = lax.dot_general(
                    select[...], jnp.concatenate(tiles, axis=1), NT, preferred_element_type=jnp.float32
                ).astype(jnp.bfloat16)
                start = first
                while start < first + 256:
                    q, line = start // lines, start % lines
                    count = min(lines - line, first + 256 - start)
                    place = q * depth + x * lines + line
                    rows_ref[:, place : place + count] = value[
                        :, start - first : start - first + count
                    ]
                    start += count

        if copies:
            before.wait()

    half = out_ref.shape[2]
    mine = pl.ds(pl.multiple_of(feed_ref[0] * half, half), half)
    cols = out_ref.shape[3]
    start = pl.multiple_of(pl.program_id(1) * cols, cols)
    other = pl.ds(start, cols)

    def dot(left, right):
        return lax.dot_general(left, right, NT, preferred_element_type=jnp.float32)

    real, imag = slice(0, depth), slice(depth, 2 * depth)
    out_re = dot(rows_ref[mine, :], rows_ref[other, :]) * norm_scale
    out_im = (
        dot(rows_ref[mine, imag], rows_ref[other, real])
        - dot(rows_ref[mine, real], rows_ref[other, imag])
    ) * norm_scale
    if copies:
        out_re = out_re + before_ref[0, :, other]
        out_im = out_im + before_ref[1, :, other]
    elif adds:
        out_re = out_re + refs[2 * pieces + 1][0, 0]
        out_im = out_im + refs[2 * pieces + 1][1, 0]
    out_ref[0, 0] = out_re
    out_ref[1, 0] = out_im


def correlate(feed, pieces, select, first, count, out_count, frames, feeds, result, adds):
    span = LANES // feeds
    total = select.shape[0]
    half = total // 2
    operands, in_specs = [], []
    for pair in pieces:
        for array in pair:
            operands.append(array)
            in_specs.append(
                pl.BlockSpec(
                    (array.shape[0], 1) + array.shape[2:], lambda o, n, feed: (0, o, 0, 0, 0, 0)
                )
            )
    depth = array.shape[3] * 16 * span
    operands.append(select)
    in_specs.append(
        pl.BlockSpec(select.shape, lambda o, n, feed: (0, 0), pipeline_mode=pl.Buffered(1))
    )
    copies = adds and count == 1
    cols = COLS // 2 if copies else COLS
    out_spec = pl.BlockSpec((2, 1, half, cols), lambda o, n, feed: (0, first + o, 0, n))
    aliases = {}
    if result is not None:
        aliases = {1 + len(operands): 0}
        operands.append(result)
        in_specs.append(out_spec if adds and not copies else pl.BlockSpec(memory_space=pl.ANY))
    scratch = [pltpu.VMEM((total, 2 * depth), jnp.bfloat16)]
    if copies:
        scratch += [pltpu.VMEM((2, half, total), jnp.float32), pltpu.SemaphoreType.DMA]
    return pl.pallas_call(
        functools.partial(
            correlate_kernel, (feeds, len(pieces), 1.0 / (frames * AVG), adds, copies, first)
        ),
        grid_spec=pltpu.PrefetchScalarGridSpec(
            num_scalar_prefetch=1,
            grid=(count, total // cols),
            in_specs=in_specs,
            out_specs=out_spec,
            scratch_shapes=scratch,
        ),
        out_shape=jax.ShapeDtypeStruct((2, out_count, half, total), jnp.float32),
        input_output_aliases=aliases,
        compiler_params=pltpu.CompilerParams(vmem_limit_bytes=40 * 1024 * 1024),
        cost_estimate=pl.CostEstimate(flops=1000, bytes_accessed=1000, transcendentals=0),
    )(feed.reshape(1), *operands)


def body(voltages, input_order):
    feeds = voltages.shape[1]
    chans = lax.axis_size("chan")
    me = lax.axis_index("chan").astype(jnp.int32)
    feed = lax.axis_index("feed").astype(jnp.int32)
    frames = voltages.shape[2] // CH - TAPS + 1
    steps = frames // STEP
    outs_per_dev = CH // chans // AVG
    window = jnp.asarray(make_window())
    table = jnp.asarray(make_table())

    sources = (
        ((feed ^ jnp.arange(2, dtype=jnp.int32)) * (chans * feeds))[:, None, None]
        + ((me ^ jnp.arange(chans, dtype=jnp.int32)) * feeds)[None, :, None]
        + jnp.arange(feeds, dtype=jnp.int32)[None, None, :]
    ).reshape(1, 2 * chans * feeds)
    select = (input_order[:, None] == sources).astype(jnp.bfloat16)

    near, far = list(range(1, chans // 2)), list(range(chans // 2, chans))
    turns = [k for pair in zip(far, near) for k in pair] + far[-1:]
    flying = []

    def send(k, block, *after):
        if len(flying) >= WINDOW:
            store, key = flying.pop(0)
            block, store[key] = lax.optimization_barrier((block, store[key]))
        if after:
            block, *after = lax.optimization_barrier((block, *after))
        store = {k: lax.ppermute(block, "chan", [(c, c ^ k) for c in range(chans)])}
        flying.append((store, k))
        return store

    def share(block, received, cuts, begin=0, count=None):
        parts = [block]
        for k in range(1, chans):
            array = received[k][k]
            whole = count is None or array.shape[0] == count
            parts.append(array if whole else array[begin : begin + count])
        pieces = []
        for low, high in zip([0] + cuts, cuts):
            own = jnp.stack(parts[low:high])
            pieces.append((own, lax.ppermute(own, "feed", [(0, 1), (1, 0)])))
        return pieces

    unit = LANES // feeds
    first = unit if steps > unit else 0
    groups = [(0, outs_per_dev)]
    if outs_per_dev > 1:
        groups = [(0, outs_per_dev - 1), (outs_per_dev - 1, 1)]
    if first:
        start_far, start = channelize(
            voltages, me, window, table, 0, first, [(0, outs_per_dev)], chans
        )
        start_far[0].update({k: start[k] for k in near})
        me, start[0] = lax.optimization_barrier((me, start[0]))
    far_blocks, near_blocks = channelize(
        voltages, me, window, table, first, steps - first, groups, chans
    )
    result = early = None
    if first:
        early = {}
        for place, k in enumerate(turns):
            block = start_far[0][k]
            if place == WINDOW:
                block, near_blocks[0] = lax.optimization_barrier((block, near_blocks[0]))
            early[k] = send(k, block)
    sent = [{k: None for k in near} for _ in groups]
    for place, k in enumerate(turns):
        block = near_blocks[k] if k in near else far_blocks[0][k]
        if first and place == len(turns) - 2:
            result = correlate(
                feed, share(start[0], early, [chans]),
                select, 0, outs_per_dev, outs_per_dev, frames, feeds, None, False,
            )
            block, result = lax.optimization_barrier((block, result))
        store = send(k, block)
        for received in sent if k in near else sent[:1]:
            received[k] = store
    for k in far if len(groups) > 1 else []:
        sent[1][k] = send(k, far_blocks[1][k])
    for g, (begin, count) in enumerate(groups):
        mine = near_blocks[0][begin : begin + count]
        if g:
            mine, result = lax.optimization_barrier((mine, result))
        result = correlate(
            feed, share(mine, sent[g], [chans], begin, count),
            select, begin, count, outs_per_dev, frames, feeds, result, first > 0,
        )
    return result


def solution(mesh):
    in_specs = (P(None, ("grp", "feed", "chan"), None), P())
    out_specs = P(None, ("grp", "chan"), "feed", None)
    return jax.shard_map(body, mesh=mesh, in_specs=in_specs, out_specs=out_specs, check_vma=False)
```
